256 devices in a mesh: ab: 16 (over y_hi, x, core), cd: 16 (over y_lo, z).
Axes of the slice: x: 4, y: 4 (y_hi: 2, y_lo: 2; y = y_hi * 2 + y_lo), z: 8, core: 2. Of those that a mesh axis runs over, the one named last changes fastest.
Arguments:
- amplitudes: float32 [384, 640000], P('cd', 'ab'), may hold values from -6 to 6
- integrals: float32 [800, 640000], P(None, ('ab', 'cd')), may hold values from -0.015625 to 0.015625
- pair_index: int32 [384], P('cd'), may hold values from 0 to 9999
- occ_energy: float32 [100], replicated, may hold values from -2 to -0.3
- virt_energy: float32 [800], replicated, may hold values from 0.2 to 4
Outputs:
- increment: float32 [384, 800], P('cd', 'ab')
The draws below stay inside these ranges and needn't reach their ends.
All inputs are finite; a program needn't handle non-finite values.
Results may differ from the reference program's by a relative error of at most 0.00012.
Values sent between devices are 32-bit elements; how exact they have to be, the bound alone decides.
A program may use at most 128 MiB of HBM per device.

```python
import jax
import jax.numpy as jnp
from jax import lax

NOCC = 100
NV = 800
IJ = 384
AB = 800
CD = 640000


def set_ends(array, rng, least, top_value):
    shape = array.shape
    place = [jax.random.randint(jax.random.fold_in(rng, axis), (), 0, shape[axis]) for axis in range(len(shape))]
    array = array.at[tuple(place)].set(least)
    longest = shape.index(max(shape))
    place[longest] = (place[longest] + 1) % shape[longest]
    return array.at[tuple(place)].set(top_value)


def spiked(drawn, own_key, source, target, blocks, factor):
    def block_of(position):
        return (jnp.arange(drawn.shape[position]) // (drawn.shape[position] // blocks)).reshape((-1,) + (1,) * (drawn.ndim - 1 - position))

    one_side = jax.random.permutation(own_key, blocks)[block_of(target)]
    other_side = (block_of(target) + blocks // 2) % blocks
    return jnp.where((block_of(source) == one_side) | (block_of(source) == other_side), factor * drawn, drawn)


def steps_of(stream_key, shape, pieces, low, high):
    def one(axis_at, shards_of):
        heights = jax.random.uniform(jax.random.fold_in(jax.random.fold_in(stream_key, 6), axis_at), (shards_of,), jnp.float32, low / len(pieces), high / len(pieces))
        return jnp.repeat(jnp.exp(heights), shape[axis_at] // shards_of).reshape((-1,) + (1,) * (len(shape) - axis_at - 1))

    level = one(*pieces[0])
    for cut in pieces[1:]:
        level = level * one(*cut)
    return level


def gaussian(key, extent, deviation, limit, cuts=(), kind=jnp.bfloat16):
    level = steps_of(key, extent, cuts, -0.22, 0.18) if cuts else 1.0
    array = jax.random.normal(key, extent, jnp.float32) * deviation * level
    return jnp.minimum(jnp.maximum(array, -limit), limit).astype(kind)


def noise_with(rng, dims, scale, bound, split, heavy, kind=jnp.bfloat16):
    drawn = scale * jax.random.normal(rng, dims, jnp.float32)
    if split:
        drawn = drawn * steps_of(rng, dims, split, -0.22, 0.18)
    return jnp.clip(spiked(drawn, jax.random.fold_in(rng, 3), *heavy), -bound, bound).astype(kind)


def setup_inputs(seed: int = 0) -> dict:
    arg_keys = jax.random.split(jax.random.key(seed), 6)
    return {
        "amplitudes": gaussian(arg_keys[0], (IJ, CD), 1.0, 6.0, ((0, 16), (1, 16)), jnp.float32),
        "integrals": noise_with(arg_keys[1], (AB, CD), CD ** -0.5, 0.015625, ((1, 256),), (1, 0, 32, 2.75), jnp.float32),
        "pair_index": set_ends(jax.random.randint(arg_keys[2], (IJ,), 0, NOCC * NOCC), jax.random.fold_in(arg_keys[2], 1), 0, (NOCC * NOCC) - 1).astype(jnp.int32),
        "occ_energy": jnp.clip(jax.random.uniform(arg_keys[3], (NOCC,), jnp.float32, -2.0, -0.3), -2.0, -0.3),
        "virt_energy": jnp.clip(jax.random.uniform(arg_keys[4], (NV,), jnp.float32, 0.2, 4.0), 0.2, 4.0),
    }


def reference(amplitudes, integrals, pair_index, occ_energy, virt_energy):
    ladder = lax.dot_general(amplitudes, integrals, (((1,), (1,)), ((), ())), precision=lax.Precision.HIGHEST, preferred_element_type=jnp.float32)
    first_occ = pair_index // NOCC
    second_occ = pair_index % NOCC
    row_ids = jnp.arange(AB, dtype=jnp.int32)
    outer_virt = row_ids // NV
    inner_virt = row_ids % NV
    occ_pair = occ_energy[first_occ] + occ_energy[second_occ]
    virt_pair = virt_energy[outer_virt] + virt_energy[inner_virt]
    denominator = occ_pair[:, None] - virt_pair[None, :]
    return ladder / denominator
```

```python
import functools

import jax
import jax.numpy as jnp
from jax import lax
from jax.experimental import pallas as pl
from jax.experimental.pallas import tpu as pltpu
from jax.sharding import PartitionSpec as P

NOCC = 100
NV = 800
MESH = pl.DeviceIdType.MESH

ROWS = 24
EACH = 2500
WIDE = 2560
TILES = WIDE // 128
FULL = EACH // 128
REST = EACH - FULL * 128
SENT = (3 * FULL + 2) * 128
COLS = 40000
WINDOW = 800
MINE = 50
LAG = 3

PLUS = ("A4", "A3", "A2", "A4", "A3", "B3", "A2", "A4", "A3", "B3", "B2", "A4", "B1", "B3", "B2", "A1")
MINUS = ("A3", "A2", "A1", "A3", "B4", "A2", "B3", "B4", "A3", "B3", "B4", "B2", "B3", "B4", "B2", "B1")
YORDER = [("m", 4), ("p", 3), ("m", 3), ("p", 2), ("m", 2), ("p", 1), ("m", 1), ("p", 0)]
BATCHES = {
    2: (("own",), ("m", 2)),
    6: (("p", 6), ("m", 5)),
    8: (("p", 8), ("m", 8)),
    11: (("p", 11), ("y", 7)),
    12: (("p", 12), ("m", 12)),
    13: (("p", 13), ("m", 13)),
    14: (("p", 14), ("m", 14)),
    15: (("p", 15), ("m", 15)),
}
NB = len(BATCHES)


def kernel(
    amp, integrals, pair_ref, occ_ref, virt_ref, out,
    amp_v, int_v, vhi, vlo, pack, ybuf, pbuf, mbuf, lhs, part, crecv, xs, xrecv, cs, crow, den,
    amp_sem, int_sem, ysend, yrecv, psend, precv, msend, mrecv, c_s, c_r, x_s, x_r, d_s, d_r,
):
    ab, cd = lax.axis_index("ab"), lax.axis_index("cd")
    core, x, yh = ab % 2, (ab // 2) % 4, ab // 8
    yl, z = cd // 8, cd % 8

    def on_ab(h, xx, c):
        return ((h * 4 + xx) * 2 + c, cd)

    def on_cd(y, zz):
        return (ab, y * 8 + zz)

    amp_copy = pltpu.make_async_copy(amp, amp_v, amp_sem)
    int_copy = pltpu.make_async_copy(integrals, int_v, int_sem)
    amp_copy.start()

    partner_core = on_ab(yh, x, 1 - core)
    partners_x = [on_ab((yh + k // 4) % 2, (x + k) % 4, core) for k in range(1, 8)]
    partner_yl = on_cd(1 - yl, z)
    others_cd = [on_cd((yl + k // 8) % 2, (z + k) % 8) for k in range(1, 16)]
    greeted = others_cd + [partner_core] + partners_x
    barrier = pltpu.get_barrier_semaphore()
    for device in greeted:
        pl.semaphore_signal(barrier, inc=1, device_id=device, device_id_type=MESH)

    lane = lax.broadcasted_iota(jnp.int32, (ROWS, 128), 1)
    lane8 = lax.broadcasted_iota(jnp.int32, (8, 128), 1)

    def owner_piece(k):
        if k == 15:
            return yl * 8 + z
        if k < 8:
            way, far = YORDER[k]
            step = far if way == "p" else 8 - far
            return (1 - yl) * 8 + (z + step) % 8
        step = k - 7 if k < 12 else 8 - (k - 11)
        return yl * 8 + (z + step) % 8

    def pack_block(k):
        piece = owner_piece(k)
        begin = piece * EACH
        tile = begin // 128
        off = begin - tile * 128
        turn = lax.rem(128 - off, 128)
        tail = jnp.concatenate(
            [amp_v[:, COLS - 64 : COLS], jnp.zeros((ROWS, 64), jnp.float32)], axis=1
        )
        keep = lane < 128 - off

        def rolled(j):
            if j < TILES:
                block = amp_v[:, pl.ds(pl.multiple_of((tile + j) * 128, 128), 128)]
            else:
                at = jnp.minimum(tile + TILES, COLS // 128 - 1)
                block = amp_v[:, pl.ds(pl.multiple_of(at * 128, 128), 128)]
                block = jnp.where(piece == 15, tail, block)
            return pltpu.roll(block, turn, 1)

        now = rolled(0)
        for j in range(FULL):
            later = rolled(j + 1)
            value = jnp.where(keep, now, later)
            for r in range(3):
                pack[k, :, (r * FULL + j) * 128 : (r * FULL + j + 1) * 128] = value[r * 8 : r * 8 + 8]
            now = later
        value = jnp.where(keep, now, rolled(FULL + 1))
        one, two, three = value[0:8], value[8:16], value[16:24]
        pack[k, :, 3 * FULL * 128 : (3 * FULL + 1) * 128] = jnp.where(lane8 < 64, one, pltpu.roll(two, 64, 1))
        over = REST - 64
        rests = jnp.where(lane8 < REST + over, pltpu.roll(one, over, 1), pltpu.roll(two, 2 * over, 1))
        rests = jnp.where(lane8 < REST + 2 * over, rests, 0.0)
        pack[k, :, (3 * FULL + 1) * 128 : SENT] = jnp.where(lane8 < REST, three, rests)

    def last_tile(ref):
        first = ref[:, 3 * FULL * 128 : (3 * FULL + 1) * 128]
        second = ref[:, (3 * FULL + 1) * 128 : SENT]
        over = REST - 64
        one = jnp.where(lane8 < 64, first, pltpu.roll(second, 128 - over, 1))
        two = jnp.where(lane8 < 64, pltpu.roll(first, 64, 1), pltpu.roll(second, 128 - 2 * over, 1))
        return [jnp.where(lane8 < REST, rest, 0.0) for rest in (one, two, second)]

    def remote(src, dst, send, recv, device):
        return pltpu.make_async_remote_copy(
            src_ref=src, dst_ref=dst, send_sem=send, recv_sem=recv, device_id=device, device_id_type=MESH
        )

    ycopies = [remote(pack.at[k], ybuf.at[k], ysend.at[k], yrecv.at[k], partner_yl) for k in range(8)]
    state = {"y_started": 0, "y_waited": 0}
    packed = set()

    def ensure_pack(k):
        if k not in packed:
            packed.add(k)
            pack_block(k)

    def y_start():
        k = state["y_started"]
        if k < 8:
            ensure_pack(k)
            ycopies[k].start()
            state["y_started"] = k + 1

    def y_wait(k):
        while state["y_waited"] <= k:
            ycopies[state["y_waited"]].wait_recv()
            state["y_waited"] += 1
            y_start()

    yrank = {key: k for k, key in enumerate(YORDER)}
    ring, needs, block_info = {}, {}, {("own",): (0, 0), ("y", 7): (1, 0)}
    for way, sequence, step, buf, send, recv in (
        ("p", PLUS, 1, pbuf, psend, precv),
        ("m", MINUS, 7, mbuf, msend, mrecv),
    ):
        device = on_cd(yl, (z + step) % 8)
        last = {}
        for slot, name in enumerate(sequence):
            far = int(name[1])
            if name in last:
                src, need = buf.at[last[name]], None
            elif name[0] == "A":
                k = 7 + far if way == "p" else 11 + far
                src, need = pack.at[k], ("pack", k)
            else:
                k = yrank[(way, far)]
                src, need = ybuf.at[k], ("y", k)
            last[name] = slot
            ring[way, slot] = remote(src, buf.at[slot], send.at[slot], recv.at[slot], device)
            needs[way, slot] = need
            block_info[way, slot] = (0 if name[0] == "A" else 1, (8 - far) % 8 if way == "p" else far)

    def ring_start(way, slot):
        if slot >= 16:
            return
        need = needs[way, slot]
        if need is not None and need[0] == "pack":
            ensure_pack(need[1])
        elif need is not None:
            y_wait(need[1])
        ring[way, slot].start()

    def split_columns(at, width):
        for place in range(0, 1024, 128):
            pieces = []
            for h in (0, 1):
                g = (h * 4 + place // 128 % 4) * 2 + place // 512
                value = int_v[g * MINE : (g + 1) * MINE, pl.ds(at, width)]
                if width < 128:
                    value = jnp.concatenate([value, jnp.zeros((MINE, 128 - width), jnp.float32)], axis=1)
                pieces += [value, jnp.zeros((64 - MINE, 128), jnp.float32)]
            value = jnp.concatenate(pieces, axis=0).T
            high = value.astype(jnp.bfloat16)
            low = (value - high.astype(jnp.float32)).astype(jnp.bfloat16)
            vhi[place // 256, pl.ds(at, 128), place % 256 : place % 256 + 128] = high
            vlo[place // 256, pl.ds(at, 128), place % 256 : place % 256 + 128] = low

    def split_range(first, end):
        def body(j, carry):
            split_columns(pl.multiple_of(j * 128, 128), 128)
            return carry

        lax.fori_loop(first, end, body, 0)

    batches = list(BATCHES.values())

    def block_ref(block):
        if block[0] == "own":
            return pack.at[15]
        if block[0] == "y":
            return ybuf.at[block[1]]
        return (pbuf if block[0] == "p" else mbuf).at[block[1]]

    core_copies = [remote(part.at[b, 1 - core], crecv.at[b], c_s.at[b], c_r.at[b], partner_core) for b in range(NB)]
    x_copies = [
        [
            remote(
                xs.at[b, (yh + k // 4) % 2 * 4 + (x + k) % 4],
                xrecv.at[b, k - 1], x_s.at[b, k - 1], x_r.at[b, k - 1], partners_x[k - 1],
            )
            for k in range(1, 8)
        ]
        for b in range(NB)
    ]
    owner_copies = {}
    for b in range(NB):
        for i, block in enumerate(batches[b]):
            if block[0] != "own":
                dy, dz = block_info[block]
                device = on_cd((yl + dy) % 2, (z + dz) % 8)
                n = b * 2 + i
                owner_copies[n] = remote(cs.at[n], crow.at[n], d_s.at[n], d_r.at[n], device)

    def multiply(b):
        one, two = (block_ref(block) for block in batches[b])

        def put(value, at, width):
            high = value.astype(jnp.bfloat16)
            lhs[0:48, at : at + width] = high
            lhs[48:96, at : at + width] = (value - high.astype(jnp.float32)).astype(jnp.bfloat16)

        for j in range(0, FULL * 128, 512):
            width = min(512, FULL * 128 - j)
            starts = [r * FULL * 128 + j for r in range(3)]
            put(jnp.concatenate([ref[:, at : at + width] for ref in (one, two) for at in starts], axis=0), j, width)
        put(jnp.concatenate(last_tile(one) + last_tile(two), axis=0), FULL * 128, 128)
        dims = (((1,), (0,)), ((), ()))
        for n in range(4):
            first = lax.dot_general(lhs[...], vhi[n], dims, preferred_element_type=jnp.float32)
            second = lax.dot_general(lhs[0:48, :], vlo[n], dims, preferred_element_type=jnp.float32)
            total = first[0:48] + first[48:96] + second
            part[b, n // 2, :, (n % 2) * 256 : (n % 2) * 256 + 256] = total

    def stage_one(b):
        multiply(b)
        core_copies[b].start()

    def stage_two(b):
        core_copies[b].wait_recv()
        for k in range(4):
            value = part[b, core, :, k * 128 : (k + 1) * 128] + crecv[b, :, k * 128 : (k + 1) * 128]
            turned = pltpu.roll(value, 64, 1)
            xs[b, k] = jnp.where(lane < 64, value[0:ROWS], turned[ROWS:])
            xs[b, 4 + k] = jnp.where(lane < 64, turned[0:ROWS], value[ROWS:])
        for copy in x_copies[b]:
            copy.start()

    def stage_three(b):
        value = xs[b, yh * 4 + x]
        for k, copy in enumerate(x_copies[b]):
            copy.wait_recv()
            value = value + xrecv[b, k]
        turned = pltpu.roll(value, 64, 1)
        for i, block in enumerate(batches[b]):
            n = b * 2 + i
            low, high = (value, turned) if i == 0 else (turned, value)
            high = jnp.concatenate([high[16:24], jnp.zeros((8, 128), jnp.float32)], axis=0)
            both = jnp.where(lane[0:16] < 64, low[0:16], high)
            if block[0] == "own":
                crow[n] = both
            else:
                cs[n] = both
                owner_copies[n].start()

    pl.semaphore_wait(barrier, len(greeted))
    amp_copy.wait()
    int_copy.start()

    y_start()
    for slot in range(LAG):
        ring_start("p", slot)
        ring_start("m", slot)
    y_start()
    for k in range(16):
        ensure_pack(k)

    row24 = lax.broadcasted_iota(jnp.int32, (ROWS, 128), 0)
    occ_pair = jnp.zeros((ROWS, 128), jnp.float32)
    for r in range(ROWS):
        pair = pair_ref[r]
        occ_pair = jnp.where(row24 == r, occ_ref[pair // NOCC] + occ_ref[pair % NOCC], occ_pair)
    virt_pair = jnp.zeros((ROWS, 128), jnp.float32)
    for c in range(MINE):
        row = ab * MINE + c
        virt_pair = jnp.where(lane == c, virt_ref[row // NV] + virt_ref[row % NV], virt_pair)
    den[...] = occ_pair - virt_pair

    int_copy.wait()
    split_columns(FULL * 128, REST)
    splits = {0: (0, 9), 1: (9, 19)}

    for slot in range(16):
        for way in ("p", "m"):
            ring[way, slot].wait_recv()
            ring_start(way, slot + LAG)
        if slot in splits:
            split_range(*splits[slot])
        if slot in BATCHES:
            b = list(BATCHES).index(slot)
            if ("y", 7) in BATCHES[slot]:
                y_wait(7)
            stage_one(b)
            if b:
                stage_three(b - 1)
            stage_two(b)

    def owner_sum(total, first, end):
        for n in range(first, end):
            if n:
                owner_copies[n].wait_recv()
            total = total + crow[n]
        return total

    total = owner_sum(jnp.zeros((16, 128), jnp.float32), 0, 2 * NB - 4)
    stage_three(NB - 1)
    total = owner_sum(total, 2 * NB - 4, 2 * NB)
    turned = pltpu.roll(total, 64, 1)
    ladder = jnp.concatenate([total, turned[0:8]], axis=0)
    out[...] = (ladder / den[...])[:, :MINE]

    for copy in ycopies + list(ring.values()) + core_copies + sum(x_copies, []) + list(owner_copies.values()):
        copy.wait_send()


def per_device(amplitudes, integrals, pair_index, occ_energy, virt_energy):
    dma = pltpu.SemaphoreType.DMA

    def f32(*shape):
        return pltpu.VMEM(shape, jnp.float32)

    def bf16(*shape):
        return pltpu.VMEM(shape, jnp.bfloat16)

    return pl.pallas_call(
        kernel,
        out_shape=jax.ShapeDtypeStruct((ROWS, MINE), jnp.float32),
        in_specs=[pl.BlockSpec(memory_space=pl.ANY)] * 2 + [pl.BlockSpec(memory_space=pltpu.SMEM)] * 3,
        out_specs=pl.BlockSpec(memory_space=pltpu.VMEM),
        scratch_shapes=[
            f32(ROWS, COLS), f32(WINDOW, EACH), bf16(4, WIDE, 256), bf16(4, WIDE, 256),
            f32(16, 8, SENT), f32(8, 8, SENT), f32(16, 8, SENT), f32(16, 8, SENT),
            bf16(96, WIDE), f32(NB, 2, 48, 512), f32(NB, 48, 512), f32(NB, 8, ROWS, 128), f32(NB, 7, ROWS, 128),
            f32(2 * NB, 16, 128), f32(2 * NB, 16, 128), f32(ROWS, 128),
            dma, dma, dma((8,)), dma((8,)), dma((16,)), dma((16,)), dma((16,)), dma((16,)),
            dma((NB,)), dma((NB,)), dma((NB, 7)), dma((NB, 7)), dma((2 * NB,)), dma((2 * NB,)),
        ],
        compiler_params=pltpu.CompilerParams(
            collective_id=0, has_side_effects=True, vmem_limit_bytes=60 * 2**20
        ),
        cost_estimate=pl.CostEstimate(flops=4_700_000_000, bytes_accessed=12_000_000, transcendentals=0),
        name="ladder",
    )(amplitudes, integrals, pair_index, occ_energy, virt_energy)


def solution(mesh):
    return jax.shard_map(
        per_device,
        mesh=mesh,
        in_specs=(P("cd", "ab"), P(None, ("ab", "cd")), P("cd"), P(), P()),
        out_specs=P("cd", "ab"),
        check_vma=False,
    )
```

```python
import functools

import jax
import jax.numpy as jnp
from jax import lax
from jax.experimental import pallas as pl
from jax.experimental.pallas import tpu as pltpu
from jax.sharding import PartitionSpec as P

NOCC = 100
NV = 800
MESH = pl.DeviceIdType.MESH

ROWS = 24
EACH = 2500
WIDE = 2560
TILES = WIDE // 128
FULL = EACH // 128
REST = EACH - FULL * 128
SENT = (3 * FULL + 2) * 128
HALF_TILES = 10
HALF = HALF_TILES * 3 * 128
COLS = 40000
WINDOW = 800
MINE = 50
LAG = 3

SEQUENCE = (
    ("A4", "half"), ("A3", "all"), ("A2", "all"), ("A4", "half"), ("A3", "all"), ("B4", "half"), ("A4", "half"),
    ("A3", "all"), ("B4", "half"), ("A4", "half"), ("B3", "all"), ("B4", "half"), ("B2", "all"), ("B3", "all"),
    ("B4", "half"), ("B2", "all"), ("B3", "all"), ("A2", "all"), ("B1", "all"), ("A1", "all"),
)
SLOTS = len(SEQUENCE)
CROSS = ("B4", "B3p", "B3m", "B2p", "B2m", "B1p", "B1m", "B0")
OWN = ("A4", "A3p", "A3m", "A2p", "A2m", "A1p", "A1m", "A0")
PLACE = {name: k for k, name in enumerate(CROSS + OWN)}
BATCHES = {
    7: ("A3p", "A3m"),
    11: ("A0", "B0"),
    14: ("A4", "B4"),
    15: ("B2p", "B2m"),
    16: ("B3p", "B3m"),
    17: ("A2p", "A2m"),
    18: ("B1p", "B1m"),
    19: ("A1p", "A1m"),
}
NB = len(BATCHES)
PAIRS = tuple(BATCHES.values())
INBOX = {name: k for k, name in enumerate(CROSS + OWN[:-1])}
SEND_ON = {
    1: ("B0",), 2: ("B4",), 3: ("B2p", "B2m", "A4"), 4: ("B3p", "B3m"), 5: ("A2p", "A2m", "A3p", "A3m"), 6: ("B1p", "B1m"),
}


def kernel(
    amp, integrals, pair, occ, virt, out,
    amp_v, int_v, vhi, vlo, pack, ybuf, pbuf, mbuf, lhs, part, crecv, xs, xrecv, sums, outbox, inbox, den, pair_ref, occ_ref, virt_ref,
    amp_sem, int_sem, table_sem, ysend, yrecv, psend, precv, msend, mrecv, c_s, c_r, x_s, x_r, d_s, d_r,
):
    ab, cd = lax.axis_index("ab"), lax.axis_index("cd")
    core, x, yh = ab % 2, (ab // 2) % 4, ab // 8
    yl, z = cd // 8, cd % 8

    def on_ab(h, xx, c):
        return ((h * 4 + xx) * 2 + c, cd)

    def on_cd(y, zz):
        return (ab, y * 8 + zz)

    amp_copy = pltpu.make_async_copy(amp, amp_v, amp_sem)
    int_copy = pltpu.make_async_copy(integrals, int_v, int_sem)
    amp_copy.start()

    partner_core = on_ab(yh, x, 1 - core)
    x_order = (6, 5, 7, 2, 4, 1, 3)
    partners_x = [on_ab((yh + k // 4) % 2, (x + k) % 4, core) for k in x_order]
    partner_yl = on_cd(1 - yl, z)
    up, down = on_cd(yl, (z + 1) % 8), on_cd(yl, (z + 7) % 8)
    greeted = [up, down, partner_yl, partner_core] + partners_x
    barrier = pltpu.get_barrier_semaphore()
    for device in greeted:
        pl.semaphore_signal(barrier, inc=1, device_id=device, device_id_type=MESH)

    lane = lax.broadcasted_iota(jnp.int32, (ROWS, 128), 1)
    lane8 = lax.broadcasted_iota(jnp.int32, (8, 128), 1)

    def owner_piece(k):
        name = (CROSS + OWN)[k]
        step = int(name[1]) if name[-1] != "m" else 8 - int(name[1])
        column = yl if name[0] == "A" else 1 - yl
        return column * 8 + (z + step) % 8

    def pack_block(k):
        piece = owner_piece(k)
        begin = piece * EACH
        tile = begin // 128
        off = begin - tile * 128
        turn = lax.rem(128 - off, 128)
        tail = jnp.concatenate(
            [amp_v[:, COLS - 64 : COLS], jnp.zeros((ROWS, 64), jnp.float32)], axis=1
        )
        keep = lane < 128 - off

        def rolled(j):
            if j < TILES:
                block = amp_v[:, pl.ds(pl.multiple_of((tile + j) * 128, 128), 128)]
            else:
                at = jnp.minimum(tile + TILES, COLS // 128 - 1)
                block = amp_v[:, pl.ds(pl.multiple_of(at * 128, 128), 128)]
                block = jnp.where(piece == 15, tail, block)
            return pltpu.roll(block, turn, 1)

        now = rolled(0)
        for j in range(FULL):
            later = rolled(j + 1)
            value = jnp.where(keep, now, later)
            for r in range(3):
                pack[k, :, (3 * j + r) * 128 : (3 * j + r + 1) * 128] = value[r * 8 : r * 8 + 8]
            now = later
        value = jnp.where(keep, now, rolled(FULL + 1))
        one, two, three = value[0:8], value[8:16], value[16:24]
        pack[k, :, 3 * FULL * 128 : (3 * FULL + 1) * 128] = jnp.where(lane8 < 64, one, pltpu.roll(two, 64, 1))
        over = REST - 64
        rests = jnp.where(lane8 < REST + over, pltpu.roll(one, over, 1), pltpu.roll(two, 2 * over, 1))
        rests = jnp.where(lane8 < REST + 2 * over, rests, 0.0)
        pack[k, :, (3 * FULL + 1) * 128 : SENT] = jnp.where(lane8 < REST, three, rests)

    def last_tile(tile_of):
        first, second = tile_of(3 * FULL), tile_of(3 * FULL + 1)
        over = REST - 64
        one = jnp.where(lane8 < 64, first, pltpu.roll(second, 128 - over, 1))
        two = jnp.where(lane8 < 64, pltpu.roll(first, 64, 1), pltpu.roll(second, 128 - 2 * over, 1))
        return [jnp.where(lane8 < REST, rest, 0.0) for rest in (one, two, second)]

    def remote(src, dst, send, recv, device):
        return pltpu.make_async_remote_copy(
            src_ref=src, dst_ref=dst, send_sem=send, recv_sem=recv, device_id=device, device_id_type=MESH
        )

    ycopies = [remote(pack.at[k], ybuf.at[k], ysend.at[k], yrecv.at[k], partner_yl) for k in range(8)]
    state = {"y_started": 0, "y_waited": 0}
    packed = set()

    def ensure_pack(k):
        if k not in packed:
            packed.add(k)
            pack_block(k)

    def y_start():
        k = state["y_started"]
        if k < 8:
            ensure_pack(k)
            ycopies[k].start()
            state["y_started"] = k + 1

    def y_wait(k):
        while state["y_waited"] <= k:
            ycopies[state["y_waited"]].wait_recv()
            state["y_waited"] += 1
            y_start()

    ring, needs, arrived = {}, {}, {}
    for way, device, buf, send, recv in (("p", up, pbuf, psend, precv), ("m", down, mbuf, msend, mrecv)):
        last = {}
        for slot, (name, size) in enumerate(SEQUENCE):
            if size == "all":
                columns = slice(0, SENT)
            elif size == "first" or (size == "half" and way == "p"):
                columns = slice(0, HALF)
            else:
                columns = slice(HALF, SENT)
            full = name if name[1] == "4" else name + way
            if name in last and size != "second":
                src, need = buf.at[last[name]], None
            else:
                k = PLACE[full]
                need = ("y", k) if k < 8 else ("pack", k)
                src = (ybuf if k < 8 else pack).at[k]
            last[name] = slot
            arrived[full, columns.start] = (way, slot)
            ring[way, slot] = remote(
                src.at[:, columns], buf.at[slot].at[:, columns], send.at[slot], recv.at[slot], device
            )
            needs[way, slot] = need

    def ring_start(way, slot):
        if slot >= SLOTS:
            return
        need = needs[way, slot]
        if need is not None and need[0] == "pack":
            ensure_pack(need[1])
        elif need is not None:
            y_wait(need[1])
        ring[way, slot].start()

    def split_columns(at, width):
        for place in range(0, 1024, 128):
            pieces = []
            for h in (0, 1):
                g = (h * 4 + place // 128 % 4) * 2 + place // 512
                value = int_v[g * MINE : (g + 1) * MINE, pl.ds(at, width)]
                if width < 128:
                    value = jnp.concatenate([value, jnp.zeros((MINE, 128 - width), jnp.float32)], axis=1)
                pieces += [value, jnp.zeros((64 - MINE, 128), jnp.float32)]
            value = jnp.concatenate(pieces, axis=0).T
            high = value.astype(jnp.bfloat16)
            low = (value - high.astype(jnp.float32)).astype(jnp.bfloat16)
            vhi[place // 256, pl.ds(at, 128), place % 256 : place % 256 + 128] = high
            vlo[place // 256, pl.ds(at, 128), place % 256 : place % 256 + 128] = low

    def split_range(first, end):
        def body(j, carry):
            split_columns(pl.multiple_of(j * 128, 128), 128)
            return carry

        lax.fori_loop(first, end, body, 0)

    def tile_reader(name):
        def tile_of(t):
            columns = slice(t * 128, t * 128 + 128)
            if name == "A0":
                return pack[PLACE[name], :, columns]
            if name == "B0":
                return ybuf[PLACE[name], :, columns]
            start = HALF if t * 128 >= HALF and (name, HALF) in arrived else 0
            way, slot = arrived[name, start]
            return (pbuf if way == "p" else mbuf)[slot, :, columns]

        return tile_of

    core_copies = [remote(part.at[b, 1 - core], crecv.at[b], c_s.at[b], c_r.at[b], partner_core) for b in range(NB)]
    x_copies = [
        [
            remote(
                xs.at[b, (yh + k // 4) % 2 * 4 + (x + k) % 4],
                xrecv.at[b, i], x_s.at[b, i], x_r.at[b, i], partners_x[i],
            )
            for i, k in enumerate(x_order)
        ]
        for b in range(NB)
    ]
    owner_copies = {}
    for name, k in INBOX.items():
        step = int(name[1]) if name[-1] == "m" else (8 - int(name[1])) % 8
        device = partner_yl if name[0] == "B" else on_cd(yl, (z + step) % 8)
        owner_copies[name] = remote(outbox.at[k], inbox.at[k], d_s.at[k], d_r.at[k], device)

    def multiply(b, first, end):
        one, two = (tile_reader(name) for name in PAIRS[b])
        for j in range(first, end):
            if j < FULL:
                pieces = [tile_of(3 * j + r) for tile_of in (one, two) for r in range(3)]
            else:
                pieces = last_tile(one) + last_tile(two)
            value = jnp.concatenate(pieces, axis=0)
            high = value.astype(jnp.bfloat16)
            lhs[0:48, j * 128 : (j + 1) * 128] = high
            lhs[48:96, j * 128 : (j + 1) * 128] = (value - high.astype(jnp.float32)).astype(jnp.bfloat16)
        dims = (((1,), (0,)), ((), ()))
        depth = slice(first * 128, end * 128)
        for k in range(4):
            half = 1 - core if k < 2 else core
            n = half * 2 + k % 2
            main = lax.dot_general(lhs[:, depth], vhi[n, depth], dims, preferred_element_type=jnp.float32)
            rest = lax.dot_general(lhs[0:48, depth], vlo[n, depth], dims, preferred_element_type=jnp.float32)
            total = main[0:48] + main[48:96] + rest
            columns = slice((k % 2) * 256, (k % 2) * 256 + 256)
            if first:
                total = total + part[b, half, :, columns]
            part[b, half, :, columns] = total
            if k == 1 and end == TILES:
                core_copies[b].start()

    def stage_two(b):
        core_copies[b].wait_recv()
        for k in range(4):
            value = part[b, core, :, k * 128 : (k + 1) * 128] + crecv[b, :, k * 128 : (k + 1) * 128]
            turned = pltpu.roll(value, 64, 1)
            xs[b, k] = jnp.where(lane < 64, value[0:ROWS], turned[ROWS:])
            xs[b, 4 + k] = jnp.where(lane < 64, turned[0:ROWS], value[ROWS:])
        for copy in x_copies[b]:
            copy.start()

    def stage_three(b):
        value = xs[b, yh * 4 + x]
        for k, copy in enumerate(x_copies[b]):
            copy.wait_recv()
            value = value + xrecv[b, k]
        turned = pltpu.roll(value, 64, 1)
        for i in (0, 1):
            low, high = (value, turned) if i == 0 else (turned, value)
            high = jnp.concatenate([high[16:24], jnp.zeros((8, 128), jnp.float32)], axis=0)
            sums[2 * b + i] = jnp.where(lane[0:16] < 64, low[0:16], high)

    def sum_of(name, inputs):
        b = [name in pair for pair in PAIRS].index(True)
        value = sums[2 * b + PAIRS[b].index(name)]
        for key in inputs:
            owner_copies[key].wait_recv()
            value = value + inbox[INBOX[key]]
        return value

    def send_on(name):
        outbox[INBOX[name]] = sum_of(name, ("B" + name[1:],) if name[0] == "A" else ())
        owner_copies[name].start()

    pl.semaphore_wait(barrier, len(greeted))
    amp_copy.wait()

    y_start()
    for slot in range(LAG):
        ring_start("p", slot)
        ring_start("m", slot)
    y_start()
    y_start()
    for k in range(16):
        ensure_pack(k)

    int_copy.start()
    tables = [
        pltpu.make_async_copy(source, table, table_sem.at[k])
        for k, (source, table) in enumerate(((pair, pair_ref), (occ, occ_ref), (virt, virt_ref)))
    ]
    for copy in tables:
        copy.start()
    for copy in tables:
        copy.wait()

    row24 = lax.broadcasted_iota(jnp.int32, (ROWS, 128), 0)
    occ_pair = jnp.zeros((ROWS, 128), jnp.float32)
    for r in range(ROWS):
        both = pair_ref[r]
        occ_pair = jnp.where(row24 == r, occ_ref[both // NOCC] + occ_ref[both % NOCC], occ_pair)
    virt_pair = jnp.zeros((ROWS, 128), jnp.float32)
    for c in range(MINE):
        row = ab * MINE + c
        virt_pair = jnp.where(lane == c, virt_ref[row // NV] + virt_ref[row % NV], virt_pair)
    den[...] = occ_pair - virt_pair

    int_copy.wait()
    split_columns(FULL * 128, REST)
    splits = {0: (0, 6), 1: (6, 12), 2: (12, 19)}

    for slot in range(SLOTS):
        for way in ("p", "m"):
            ring[way, slot].wait_recv()
            ring_start(way, slot + LAG)
        if slot in splits:
            split_range(*splits[slot])
        if slot == SLOTS - 1:
            multiply(NB - 1, 0, TILES)
            stage_three(NB - 2)
            for name in SEND_ON[NB - 2]:
                send_on(name)
            stage_two(NB - 1)
        elif slot in BATCHES:
            b = list(BATCHES).index(slot)
            if "B0" in BATCHES[slot]:
                y_wait(7)
            multiply(b, 0, TILES)
            if b:
                stage_three(b - 1)
                for name in SEND_ON.get(b - 1, ()):
                    send_on(name)
            stage_two(b)

    stage_three(NB - 1)
    send_on("A1p")
    send_on("A1m")
    total = sum_of("A0", ("B0",) + OWN[:-1])
    turned = pltpu.roll(total, 64, 1)
    ladder = jnp.concatenate([total, turned[0:8]], axis=0)
    out[...] = (ladder / den[...])[:, :MINE]

    for copy in ycopies + list(ring.values()) + core_copies + sum(x_copies, []) + list(owner_copies.values()):
        copy.wait_send()


def per_device(amplitudes, integrals, pair_index, occ_energy, virt_energy):
    dma = pltpu.SemaphoreType.DMA

    def f32(*shape):
        return pltpu.VMEM(shape, jnp.float32)

    def bf16(*shape):
        return pltpu.VMEM(shape, jnp.bfloat16)

    return pl.pallas_call(
        kernel,
        out_shape=jax.ShapeDtypeStruct((ROWS, MINE), jnp.float32),
        in_specs=[pl.BlockSpec(memory_space=pl.ANY)] * 5,
        out_specs=pl.BlockSpec(memory_space=pltpu.VMEM),
        scratch_shapes=[
            f32(ROWS, COLS), f32(WINDOW, EACH), bf16(4, WIDE, 256), bf16(4, WIDE, 256),
            f32(16, 8, SENT), f32(8, 8, SENT), f32(SLOTS, 8, SENT), f32(SLOTS, 8, SENT),
            bf16(96, WIDE), f32(NB, 2, 48, 512), f32(NB, 48, 512), f32(NB, 8, ROWS, 128), f32(NB, 7, ROWS, 128),
            f32(2 * NB, 16, 128), f32(len(INBOX), 16, 128), f32(len(INBOX), 16, 128), f32(ROWS, 128),
            pltpu.SMEM((ROWS,), jnp.int32), pltpu.SMEM((NOCC,), jnp.float32), pltpu.SMEM((NV,), jnp.float32),
            dma, dma, dma((3,)), dma((8,)), dma((8,)), dma((SLOTS,)), dma((SLOTS,)), dma((SLOTS,)), dma((SLOTS,)),
            dma((NB,)), dma((NB,)), dma((NB, 7)), dma((NB, 7)), dma((len(INBOX),)), dma((len(INBOX),)),
        ],
        compiler_params=pltpu.CompilerParams(
            collective_id=0, has_side_effects=True, vmem_limit_bytes=60 * 2**20
        ),
        cost_estimate=pl.CostEstimate(flops=4_700_000_000, bytes_accessed=12_000_000, transcendentals=0),
        name="ladder",
    )(amplitudes, integrals, pair_index, occ_energy, virt_energy)


def solution(mesh):
    return jax.shard_map(
        per_device,
        mesh=mesh,
        in_specs=(P("cd", "ab"), P(None, ("ab", "cd")), P("cd"), P(), P()),
        out_specs=P("cd", "ab"),
        check_vma=False,
    )
```

```python
import functools

import jax
import jax.numpy as jnp
from jax import lax
from jax.experimental import pallas as pl
from jax.experimental.pallas import tpu as pltpu
from jax.sharding import PartitionSpec as P

NOCC = 100
NV = 800
MESH = pl.DeviceIdType.MESH

ROWS = 24
EACH = 2500
WIDE = 2560
TILES = WIDE // 128
FULL = EACH // 128
REST = EACH - FULL * 128
SENT = (3 * FULL + 2) * 128
HALF = 10 * 3 * 128
COLS = 40000
WINDOW = 800
MINE = 50
LAG = 3

SEQUENCE = (
    ("A4", "half"), ("A3", "all"), ("A2", "all"), ("A4", "half"), ("A3", "all"), ("B4", "half"), ("A4", "half"),
    ("A3", "all"), ("B4", "half"), ("A4", "half"), ("B3", "all"), ("B4", "half"), ("B2", "all"), ("B3", "all"),
    ("B4", "half"), ("B2", "all"), ("B3", "all"), ("A2", "all"), ("B1", "all"), ("A1", "all"),
)
SLOTS = len(SEQUENCE)
CROSS = ("B4", "B3p", "B3m", "B2p", "B2m", "B1p", "B1m", "B0")
OWN = ("A4", "A3p", "A3m", "A2p", "A2m", "A1p", "A1m", "A0")
PLACE = {name: k for k, name in enumerate(CROSS + OWN)}
BATCHES = {
    7: ("A3p", "A3m"),
    11: ("A0", "B0"),
    14: ("A4", "B4"),
    15: ("B2p", "B2m"),
    16: ("B3p", "B3m"),
    17: ("A2p", "A2m"),
    18: ("B1p", "B1m"),
    19: ("A1p", "A1m"),
}
NB = len(BATCHES)
PAIRS = tuple(BATCHES.values())
INBOX = {name: k for k, name in enumerate(CROSS + OWN[:-1])}
SEND_ON = {
    1: ("B0",), 2: ("B4",), 3: ("B2p", "B2m", "A4"), 4: ("B3p", "B3m"), 5: ("A2p", "A2m", "A3p", "A3m"), 6: ("B1p", "B1m"),
}


def kernel(
    amp, integrals, pair, occ, virt, out,
    amp_v, int_v, vhi, vlo, pack, ybuf, pbuf, mbuf, lhs, part, crecv, xs, xrecv, sums, outbox, inbox, den, pair_ref, occ_ref, virt_ref,
    amp_sem, int_sem, table_sem, ysend, yrecv, psend, precv, msend, mrecv, c_s, c_r, x_s, x_r, d_s, d_r,
):
    ab, cd = lax.axis_index("ab"), lax.axis_index("cd")
    core, x, yh = ab % 2, (ab // 2) % 4, ab // 8
    yl, z = cd // 8, cd % 8

    def on_ab(h, xx, c):
        return ((h * 4 + xx) * 2 + c, cd)

    def on_cd(y, zz):
        return (ab, y * 8 + zz)

    amp_copy = pltpu.make_async_copy(amp, amp_v, amp_sem)
    int_copy = pltpu.make_async_copy(integrals, int_v, int_sem)
    amp_copy.start()

    partner_core = on_ab(yh, x, 1 - core)
    x_order = (6, 5, 7, 2, 4, 1, 3)
    partners_x = [on_ab((yh + k // 4) % 2, (x + k) % 4, core) for k in x_order]
    partner_yl = on_cd(1 - yl, z)
    up, down = on_cd(yl, (z + 1) % 8), on_cd(yl, (z + 7) % 8)
    greeted = [up, down, partner_yl, partner_core] + partners_x
    barrier = pltpu.get_barrier_semaphore()
    for device in greeted:
        pl.semaphore_signal(barrier, inc=1, device_id=device, device_id_type=MESH)

    lane = lax.broadcasted_iota(jnp.int32, (ROWS, 128), 1)
    lane8 = lax.broadcasted_iota(jnp.int32, (8, 128), 1)

    def owner_piece(k):
        name = (CROSS + OWN)[k]
        step = int(name[1]) if name[-1] != "m" else 8 - int(name[1])
        column = yl if name[0] == "A" else 1 - yl
        return column * 8 + (z + step) % 8

    def pack_block(k):
        piece = owner_piece(k)
        begin = piece * EACH
        tile = begin // 128
        off = begin - tile * 128
        turn = lax.rem(128 - off, 128)
        tail = jnp.concatenate(
            [amp_v[:, COLS - 64 : COLS], jnp.zeros((ROWS, 64), jnp.float32)], axis=1
        )
        keep = lane < 128 - off

        def rolled(j):
            if j < TILES:
                block = amp_v[:, pl.ds(pl.multiple_of((tile + j) * 128, 128), 128)]
            else:
                at = jnp.minimum(tile + TILES, COLS // 128 - 1)
                block = amp_v[:, pl.ds(pl.multiple_of(at * 128, 128), 128)]
                block = jnp.where(piece == 15, tail, block)
            return pltpu.roll(block, turn, 1)

        now = rolled(0)
        for j in range(FULL):
            later = rolled(j + 1)
            value = jnp.where(keep, now, later)
            for r in range(3):
                pack[k, :, (3 * j + r) * 128 : (3 * j + r + 1) * 128] = value[r * 8 : r * 8 + 8]
            now = later
        value = jnp.where(keep, now, rolled(FULL + 1))
        one, two, three = value[0:8], value[8:16], value[16:24]
        pack[k, :, 3 * FULL * 128 : (3 * FULL + 1) * 128] = jnp.where(lane8 < 64, one, pltpu.roll(two, 64, 1))
        over = REST - 64
        rests = jnp.where(lane8 < REST + over, pltpu.roll(one, over, 1), pltpu.roll(two, 2 * over, 1))
        rests = jnp.where(lane8 < REST + 2 * over, rests, 0.0)
        pack[k, :, (3 * FULL + 1) * 128 : SENT] = jnp.where(lane8 < REST, three, rests)

    def last_tile(tile_of):
        first, second = tile_of(3 * FULL), tile_of(3 * FULL + 1)
        over = REST - 64
        one = jnp.where(lane8 < 64, first, pltpu.roll(second, 128 - over, 1))
        two = jnp.where(lane8 < 64, pltpu.roll(first, 64, 1), pltpu.roll(second, 128 - 2 * over, 1))
        return [jnp.where(lane8 < REST, rest, 0.0) for rest in (one, two, second)]

    def remote(src, dst, send, recv, device):
        return pltpu.make_async_remote_copy(
            src_ref=src, dst_ref=dst, send_sem=send, recv_sem=recv, device_id=device, device_id_type=MESH
        )

    ycopies = [remote(pack.at[k], ybuf.at[k], ysend.at[k], yrecv.at[k], partner_yl) for k in range(8)]
    state = {"y_started": 0, "y_waited": 0}
    packed = set()

    def ensure_pack(k):
        if k not in packed:
            packed.add(k)
            pack_block(k)

    def y_start():
        k = state["y_started"]
        if k < 8:
            ensure_pack(k)
            ycopies[k].start()
            state["y_started"] = k + 1

    def y_wait(k):
        while state["y_waited"] <= k:
            ycopies[state["y_waited"]].wait_recv()
            state["y_waited"] += 1
            y_start()

    ring, needs, arrived = {}, {}, {}
    for way, device, buf, send, recv in (("p", up, pbuf, psend, precv), ("m", down, mbuf, msend, mrecv)):
        last = {}
        for slot, (name, size) in enumerate(SEQUENCE):
            if size == "all":
                columns = slice(0, SENT)
            elif way == "p":
                columns = slice(0, HALF)
            else:
                columns = slice(HALF, SENT)
            full = name if name[1] == "4" else name + way
            if name in last:
                src, need = buf.at[last[name]], None
            else:
                k = PLACE[full]
                need = ("y", k) if k < 8 else ("pack", k)
                src = (ybuf if k < 8 else pack).at[k]
            last[name] = slot
            arrived[full, columns.start] = (way, slot)
            ring[way, slot] = remote(
                src.at[:, columns], buf.at[slot].at[:, columns], send.at[slot], recv.at[slot], device
            )
            needs[way, slot] = need

    def ring_start(way, slot):
        if slot >= SLOTS:
            return
        need = needs[way, slot]
        if need is not None and need[0] == "pack":
            ensure_pack(need[1])
        elif need is not None:
            y_wait(need[1])
        ring[way, slot].start()

    def split_columns(at, width):
        for place in range(0, 1024, 128):
            pieces = []
            for h in (0, 1):
                g = (h * 4 + place // 128 % 4) * 2 + place // 512
                value = int_v[g * MINE : (g + 1) * MINE, pl.ds(at, width)]
                if width < 128:
                    value = jnp.concatenate([value, jnp.zeros((MINE, 128 - width), jnp.float32)], axis=1)
                pieces += [value, jnp.zeros((64 - MINE, 128), jnp.float32)]
            value = jnp.concatenate(pieces, axis=0).T
            high = value.astype(jnp.bfloat16)
            low = (value - high.astype(jnp.float32)).astype(jnp.bfloat16)
            vhi[place // 256, pl.ds(at, 128), place % 256 : place % 256 + 128] = high
            vlo[place // 256, pl.ds(at, 128), place % 256 : place % 256 + 128] = low

    def split_range(first, end):
        def body(j, carry):
            split_columns(pl.multiple_of(j * 128, 128), 128)
            return carry

        lax.fori_loop(first, end, body, 0)

    def tile_reader(name):
        def tile_of(t):
            columns = slice(t * 128, t * 128 + 128)
            if name == "A0":
                return pack[PLACE[name], :, columns]
            if name == "B0":
                return ybuf[PLACE[name], :, columns]
            start = HALF if t * 128 >= HALF and (name, HALF) in arrived else 0
            way, slot = arrived[name, start]
            return (pbuf if way == "p" else mbuf)[slot, :, columns]

        return tile_of

    core_copies = [remote(part.at[b, 1 - core], crecv.at[b], c_s.at[b], c_r.at[b], partner_core) for b in range(NB)]
    x_copies = [
        [
            remote(
                xs.at[b, (yh + k // 4) % 2 * 4 + (x + k) % 4],
                xrecv.at[b, i], x_s.at[b, i], x_r.at[b, i], partners_x[i],
            )
            for i, k in enumerate(x_order)
        ]
        for b in range(NB)
    ]
    owner_copies = {}
    for name, k in INBOX.items():
        step = int(name[1]) if name[-1] == "m" else (8 - int(name[1])) % 8
        device = partner_yl if name[0] == "B" else on_cd(yl, (z + step) % 8)
        owner_copies[name] = remote(outbox.at[k], inbox.at[k], d_s.at[k], d_r.at[k], device)

    def multiply(b, first, end):
        one, two = (tile_reader(name) for name in PAIRS[b])
        for j in range(first, end):
            if j < FULL:
                pieces = [tile_of(3 * j + r) for tile_of in (one, two) for r in range(3)]
            else:
                pieces = last_tile(one) + last_tile(two)
            value = jnp.concatenate(pieces, axis=0)
            high = value.astype(jnp.bfloat16)
            lhs[0:48, j * 128 : (j + 1) * 128] = high
            lhs[48:96, j * 128 : (j + 1) * 128] = (value - high.astype(jnp.float32)).astype(jnp.bfloat16)
        dims = (((1,), (0,)), ((), ()))
        depth = slice(first * 128, end * 128)
        for k in range(4):
            half = 1 - core if k < 2 else core
            n = half * 2 + k % 2
            main = lax.dot_general(lhs[:, depth], vhi[n, depth], dims, preferred_element_type=jnp.float32)
            rest = lax.dot_general(lhs[0:48, depth], vlo[n, depth], dims, preferred_element_type=jnp.float32)
            total = main[0:48] + main[48:96] + rest
            columns = slice((k % 2) * 256, (k % 2) * 256 + 256)
            if first:
                total = total + part[b, half, :, columns]
            part[b, half, :, columns] = total
            if k == 1 and end == TILES:
                core_copies[b].start()

    def stage_two(b):
        core_copies[b].wait_recv()
        for k in range(4):
            value = part[b, core, :, k * 128 : (k + 1) * 128] + crecv[b, :, k * 128 : (k + 1) * 128]
            turned = pltpu.roll(value, 64, 1)
            xs[b, k] = jnp.where(lane < 64, value[0:ROWS], turned[ROWS:])
            xs[b, 4 + k] = jnp.where(lane < 64, turned[0:ROWS], value[ROWS:])
        for copy in x_copies[b]:
            copy.start()

    def stage_three(b):
        value = xs[b, yh * 4 + x]
        for k, copy in enumerate(x_copies[b]):
            copy.wait_recv()
            value = value + xrecv[b, k]
        turned = pltpu.roll(value, 64, 1)
        for i in (0, 1):
            low, high = (value, turned) if i == 0 else (turned, value)
            high = jnp.concatenate([high[16:24], jnp.zeros((8, 128), jnp.float32)], axis=0)
            sums[2 * b + i] = jnp.where(lane[0:16] < 64, low[0:16], high)

    def sum_of(name, inputs):
        b = [name in pair for pair in PAIRS].index(True)
        value = sums[2 * b + PAIRS[b].index(name)]
        for key in inputs:
            owner_copies[key].wait_recv()
            value = value + inbox[INBOX[key]]
        return value

    def send_on(name):
        outbox[INBOX[name]] = sum_of(name, ("B" + name[1:],) if name[0] == "A" else ())
        owner_copies[name].start()
        sent.append(name)

    amp_copy.wait()
    ensure_pack(PLACE["A4"])
    pl.semaphore_wait(barrier, len(greeted))

    for slot in range(LAG):
        ring_start("p", slot)
        ring_start("m", slot)
        y_start()
    for k in range(16):
        ensure_pack(k)

    int_copy.start()
    tables = [
        pltpu.make_async_copy(source, table, table_sem.at[k])
        for k, (source, table) in enumerate(((pair, pair_ref), (occ, occ_ref), (virt, virt_ref)))
    ]
    for copy in tables:
        copy.start()
    for copy in tables:
        copy.wait()

    row24 = lax.broadcasted_iota(jnp.int32, (ROWS, 128), 0)
    occ_pair = jnp.zeros((ROWS, 128), jnp.float32)
    for r in range(ROWS):
        both = pair_ref[r]
        occ_pair = jnp.where(row24 == r, occ_ref[both // NOCC] + occ_ref[both % NOCC], occ_pair)
    virt_pair = jnp.zeros((ROWS, 128), jnp.float32)
    for c in range(MINE):
        row = ab * MINE + c
        virt_pair = jnp.where(lane == c, virt_ref[row // NV] + virt_ref[row % NV], virt_pair)
    den[...] = occ_pair - virt_pair

    int_copy.wait()
    split_columns(FULL * 128, REST)
    splits = {0: (0, 6), 1: (6, 12), 2: (12, 19)}

    waits = {"ring": 0, "batch": 0, "cross": 0}
    sent = []

    def settle(slot, batch):
        while waits["ring"] <= slot:
            for way in ("p", "m"):
                ring[way, waits["ring"]].wait_send()
            waits["ring"] += 1
        while waits["cross"] < state["y_waited"] - 1:
            ycopies[waits["cross"]].wait_send()
            waits["cross"] += 1
        while waits["batch"] <= batch:
            for copy in [core_copies[waits["batch"]]] + x_copies[waits["batch"]]:
                copy.wait_send()
            waits["batch"] += 1

    for slot in range(SLOTS):
        for way in ("p", "m"):
            ring[way, slot].wait_recv()
            ring_start(way, slot + LAG)
        if slot in splits:
            split_range(*splits[slot])
        if slot in BATCHES:
            b = list(BATCHES).index(slot)
            if "B0" in BATCHES[slot]:
                y_wait(7)
            multiply(b, 0, TILES)
            if b == NB - 1:
                stage_two(b)
            if b:
                stage_three(b - 1)
                for name in SEND_ON.get(b - 1, ()):
                    send_on(name)
            if b < NB - 1:
                stage_two(b)
                settle(slot - 3, b - 2)
        else:
            settle(slot - 3, -1)

    for name in sent[:-2]:
        owner_copies[name].wait_send()
    settle(SLOTS - 4, NB - 3)
    total = sum_of("A0", ("B0",) + OWN[:-3])
    stage_three(NB - 1)
    send_on("A1p")
    send_on("A1m")
    settle(SLOTS - 1, NB - 1)
    for copy in ycopies[waits["cross"] :] + [owner_copies[name] for name in sent[-4:]]:
        copy.wait_send()
    for name in ("A1p", "A1m"):
        owner_copies[name].wait_recv()
        total = total + inbox[INBOX[name]]
    turned = pltpu.roll(total, 64, 1)
    ladder = jnp.concatenate([total, turned[0:8]], axis=0)
    out[...] = (ladder / den[...])[:, :MINE]


def per_device(amplitudes, integrals, pair_index, occ_energy, virt_energy):
    dma = pltpu.SemaphoreType.DMA

    def f32(*shape):
        return pltpu.VMEM(shape, jnp.float32)

    def bf16(*shape):
        return pltpu.VMEM(shape, jnp.bfloat16)

    return pl.pallas_call(
        kernel,
        out_shape=jax.ShapeDtypeStruct((ROWS, MINE), jnp.float32),
        in_specs=[pl.BlockSpec(memory_space=pl.ANY)] * 5,
        out_specs=pl.BlockSpec(memory_space=pltpu.VMEM),
        scratch_shapes=[
            f32(ROWS, COLS), f32(WINDOW, EACH), bf16(4, WIDE, 256), bf16(4, WIDE, 256),
            f32(16, 8, SENT), f32(8, 8, SENT), f32(SLOTS, 8, SENT), f32(SLOTS, 8, SENT),
            bf16(96, WIDE), f32(NB, 2, 48, 512), f32(NB, 48, 512), f32(NB, 8, ROWS, 128), f32(NB, 7, ROWS, 128),
            f32(2 * NB, 16, 128), f32(len(INBOX), 16, 128), f32(len(INBOX), 16, 128), f32(ROWS, 128),
            pltpu.SMEM((ROWS,), jnp.int32), pltpu.SMEM((NOCC,), jnp.float32), pltpu.SMEM((NV,), jnp.float32),
            dma, dma, dma((3,)), dma((8,)), dma((8,)), dma((SLOTS,)), dma((SLOTS,)), dma((SLOTS,)), dma((SLOTS,)),
            dma((NB,)), dma((NB,)), dma((NB, 7)), dma((NB, 7)), dma((len(INBOX),)), dma((len(INBOX),)),
        ],
        compiler_params=pltpu.CompilerParams(
            collective_id=0, has_side_effects=True, vmem_limit_bytes=60 * 2**20
        ),
        cost_estimate=pl.CostEstimate(flops=4_700_000_000, bytes_accessed=12_000_000, transcendentals=0),
        name="ladder",
    )(amplitudes, integrals, pair_index, occ_energy, virt_energy)


def solution(mesh):
    return jax.shard_map(
        per_device,
        mesh=mesh,
        in_specs=(P("cd", "ab"), P(None, ("ab", "cd")), P("cd"), P(), P()),
        out_specs=P("cd", "ab"),
        check_vma=False,
    )
```

```python
import functools

import jax
import jax.numpy as jnp
from jax import lax
from jax.experimental import pallas as pl
from jax.experimental.pallas import tpu as pltpu
from jax.sharding import PartitionSpec as P

NOCC = 100
NV = 800
MESH = pl.DeviceIdType.MESH

ROWS = 24
EACH = 2500
WIDE = 2560
TILES = WIDE // 128
FULL = EACH // 128
REST = EACH - FULL * 128
SENT = (3 * FULL + 2) * 128
HALF = 10 * 3 * 128
COLS = 40000
WINDOW = 800
MINE = 50
LAG = 2

SEQUENCE = (
    ("A4", "half"), ("A3", "all"), ("A2", "all"), ("A4", "half"), ("A3", "all"), ("B4", "half"), ("A4", "half"),
    ("A3", "all"), ("B4", "half"), ("A4", "half"), ("B3", "all"), ("B4", "half"), ("B2", "all"), ("B3", "all"),
    ("B4", "half"), ("B2", "all"), ("B3", "all"), ("A2", "all"), ("B1", "all"), ("A1", "all"),
)
SLOTS = len(SEQUENCE)
CROSS = ("B4", "B3p", "B3m", "B2p", "B2m", "B1p", "B1m", "B0")
OWN = ("A4", "A3p", "A3m", "A2p", "A2m", "A1p", "A1m", "A0")
PLACE = {name: k for k, name in enumerate(CROSS + OWN)}
BATCHES = {
    7: ("A3p", "A3m"),
    11: ("A0", "B0"),
    14: ("A4", "B4"),
    15: ("B2p", "B2m"),
    16: ("B3p", "B3m"),
    17: ("A2p", "A2m"),
    18: ("B1p", "B1m"),
    19: ("A1p", "A1m"),
}
NB = len(BATCHES)
PAIRS = tuple(BATCHES.values())
INBOX = {name: k for k, name in enumerate(CROSS + OWN[:-1])}
SEND_ON = {
    1: ("B0",), 2: ("B4",), 3: ("B2p", "B2m", "A4"), 4: ("B3p", "B3m"), 5: ("A2p", "A2m", "A3p", "A3m"), 6: ("B1p", "B1m"),
}


def kernel(
    amp, integrals, pair, occ, virt, out,
    amp_v, int_v, vhi, vlo, pack, ybuf, pbuf, mbuf, lhs, part, crecv, xs, xrecv, sums, outbox, inbox, den, pair_ref, occ_ref, virt_ref,
    amp_sem, int_sem, table_sem, ysend, yrecv, psend, precv, msend, mrecv, c_s, c_r, x_s, x_r, d_s, d_r,
):
    ab, cd = lax.axis_index("ab"), lax.axis_index("cd")
    core, x, yh = ab % 2, (ab // 2) % 4, ab // 8
    yl, z = cd // 8, cd % 8

    def on_ab(h, xx, c):
        return ((h * 4 + xx) * 2 + c, cd)

    def on_cd(y, zz):
        return (ab, y * 8 + zz)

    amp_copy = pltpu.make_async_copy(amp, amp_v, amp_sem)
    int_copy = pltpu.make_async_copy(integrals, int_v, int_sem)
    amp_copy.start()

    partner_core = on_ab(yh, x, 1 - core)
    x_order = (6, 5, 7, 2, 4, 1, 3)
    partners_x = [on_ab((yh + k // 4) % 2, (x + k) % 4, core) for k in x_order]
    partner_yl = on_cd(1 - yl, z)
    up, down = on_cd(yl, (z + 1) % 8), on_cd(yl, (z + 7) % 8)
    greeted = [up, down, partner_yl, partner_core] + partners_x
    barrier = pltpu.get_barrier_semaphore()
    for device in greeted:
        pl.semaphore_signal(barrier, inc=1, device_id=device, device_id_type=MESH)

    lane = lax.broadcasted_iota(jnp.int32, (ROWS, 128), 1)
    lane8 = lax.broadcasted_iota(jnp.int32, (8, 128), 1)

    def owner_piece(k):
        name = (CROSS + OWN)[k]
        step = int(name[1]) if name[-1] != "m" else 8 - int(name[1])
        column = yl if name[0] == "A" else 1 - yl
        return column * 8 + (z + step) % 8

    def pack_block(k):
        piece = owner_piece(k)
        begin = piece * EACH
        tile = begin // 128
        off = begin - tile * 128
        turn = lax.rem(128 - off, 128)
        tail = jnp.concatenate(
            [amp_v[:, COLS - 64 : COLS], jnp.zeros((ROWS, 64), jnp.float32)], axis=1
        )
        keep = lane < 128 - off

        def rolled(j):
            if j < TILES:
                block = amp_v[:, pl.ds(pl.multiple_of((tile + j) * 128, 128), 128)]
            else:
                at = jnp.minimum(tile + TILES, COLS // 128 - 1)
                block = amp_v[:, pl.ds(pl.multiple_of(at * 128, 128), 128)]
                block = jnp.where(piece == 15, tail, block)
            return pltpu.roll(block, turn, 1)

        now = rolled(0)
        for j in range(FULL):
            later = rolled(j + 1)
            value = jnp.where(keep, now, later)
            for r in range(3):
                pack[k, :, (3 * j + r) * 128 : (3 * j + r + 1) * 128] = value[r * 8 : r * 8 + 8]
            now = later
        value = jnp.where(keep, now, rolled(FULL + 1))
        one, two, three = value[0:8], value[8:16], value[16:24]
        pack[k, :, 3 * FULL * 128 : (3 * FULL + 1) * 128] = jnp.where(lane8 < 64, one, pltpu.roll(two, 64, 1))
        over = REST - 64
        rests = jnp.where(lane8 < REST + over, pltpu.roll(one, over, 1), pltpu.roll(two, 2 * over, 1))
        rests = jnp.where(lane8 < REST + 2 * over, rests, 0.0)
        pack[k, :, (3 * FULL + 1) * 128 : SENT] = jnp.where(lane8 < REST, three, rests)

    def last_tile(tile_of):
        first, second = tile_of(3 * FULL), tile_of(3 * FULL + 1)
        over = REST - 64
        one = jnp.where(lane8 < 64, first, pltpu.roll(second, 128 - over, 1))
        two = jnp.where(lane8 < 64, pltpu.roll(first, 64, 1), pltpu.roll(second, 128 - 2 * over, 1))
        return [jnp.where(lane8 < REST, rest, 0.0) for rest in (one, two, second)]

    def remote(src, dst, send, recv, device):
        return pltpu.make_async_remote_copy(
            src_ref=src, dst_ref=dst, send_sem=send, recv_sem=recv, device_id=device, device_id_type=MESH
        )

    ycopies = [remote(pack.at[k], ybuf.at[k], ysend.at[k], yrecv.at[k], partner_yl) for k in range(8)]
    state = {"y_started": 0, "y_waited": 0}
    packed = set()

    def ensure_pack(k):
        if k not in packed:
            packed.add(k)
            pack_block(k)

    def y_start():
        k = state["y_started"]
        if k < 8:
            ensure_pack(k)
            ycopies[k].start()
            state["y_started"] = k + 1

    def y_wait(k):
        while state["y_waited"] <= k:
            ycopies[state["y_waited"]].wait_recv()
            state["y_waited"] += 1
            y_start()

    ring, needs, arrived = {}, {}, {}
    for way, device, buf, send, recv in (("p", up, pbuf, psend, precv), ("m", down, mbuf, msend, mrecv)):
        last = {}
        for slot, (name, size) in enumerate(SEQUENCE):
            if size == "all":
                columns = slice(0, SENT)
            elif way == "p":
                columns = slice(0, HALF)
            else:
                columns = slice(HALF, SENT)
            full = name if name[1] == "4" else name + way
            if name in last:
                src, need = buf.at[last[name]], None
            else:
                k = PLACE[full]
                need = ("y", k) if k < 8 else ("pack", k)
                src = (ybuf if k < 8 else pack).at[k]
            last[name] = slot
            arrived[full, columns.start] = (way, slot)
            ring[way, slot] = remote(
                src.at[:, columns], buf.at[slot].at[:, columns], send.at[slot], recv.at[slot], device
            )
            needs[way, slot] = need

    def ring_start(way, slot):
        if slot >= SLOTS:
            return
        need = needs[way, slot]
        if need is not None and need[0] == "pack":
            ensure_pack(need[1])
        elif need is not None:
            y_wait(need[1])
        ring[way, slot].start()

    def split_columns(at, width):
        for place in range(0, 1024, 128):
            pieces = []
            for h in (0, 1):
                g = (h * 4 + place // 128 % 4) * 2 + place // 512
                value = int_v[g * MINE : (g + 1) * MINE, pl.ds(at, width)]
                if width < 128:
                    value = jnp.concatenate([value, jnp.zeros((MINE, 128 - width), jnp.float32)], axis=1)
                pieces += [value, jnp.zeros((64 - MINE, 128), jnp.float32)]
            value = jnp.concatenate(pieces, axis=0).T
            high = value.astype(jnp.bfloat16)
            low = (value - high.astype(jnp.float32)).astype(jnp.bfloat16)
            vhi[place // 256, pl.ds(at, 128), place % 256 : place % 256 + 128] = high
            vlo[place // 256, pl.ds(at, 128), place % 256 : place % 256 + 128] = low

    def split_range(first, end):
        def body(j, carry):
            split_columns(pl.multiple_of(j * 128, 128), 128)
            return carry

        lax.fori_loop(first, end, body, 0)

    def tile_reader(name):
        def tile_of(t):
            columns = slice(t * 128, t * 128 + 128)
            if name == "A0":
                return pack[PLACE[name], :, columns]
            if name == "B0":
                return ybuf[PLACE[name], :, columns]
            start = HALF if t * 128 >= HALF and (name, HALF) in arrived else 0
            way, slot = arrived[name, start]
            return (pbuf if way == "p" else mbuf)[slot, :, columns]

        return tile_of

    core_copies = [remote(part.at[b, 1 - core], crecv.at[b], c_s.at[b], c_r.at[b], partner_core) for b in range(NB)]
    x_copies = [
        [
            remote(
                xs.at[b, (yh + k // 4) % 2 * 4 + (x + k) % 4],
                xrecv.at[b, i], x_s.at[b, i], x_r.at[b, i], partners_x[i],
            )
            for i, k in enumerate(x_order)
        ]
        for b in range(NB)
    ]
    owner_copies = {}
    for name, k in INBOX.items():
        step = int(name[1]) if name[-1] == "m" else (8 - int(name[1])) % 8
        device = partner_yl if name[0] == "B" else on_cd(yl, (z + step) % 8)
        owner_copies[name] = remote(outbox.at[k], inbox.at[k], d_s.at[k], d_r.at[k], device)

    def multiply(b, first, end):
        one, two = (tile_reader(name) for name in PAIRS[b])
        for j in range(first, end):
            if j < FULL:
                pieces = [tile_of(3 * j + r) for tile_of in (one, two) for r in range(3)]
            else:
                pieces = last_tile(one) + last_tile(two)
            value = jnp.concatenate(pieces, axis=0)
            high = value.astype(jnp.bfloat16)
            lhs[0:48, j * 128 : (j + 1) * 128] = high
            lhs[48:96, j * 128 : (j + 1) * 128] = (value - high.astype(jnp.float32)).astype(jnp.bfloat16)
        dims = (((1,), (0,)), ((), ()))
        depth = slice(first * 128, end * 128)
        for k in range(4):
            half = 1 - core if k < 2 else core
            n = half * 2 + k % 2
            main = lax.dot_general(lhs[:, depth], vhi[n, depth], dims, preferred_element_type=jnp.float32)
            rest = lax.dot_general(lhs[0:48, depth], vlo[n, depth], dims, preferred_element_type=jnp.float32)
            total = main[0:48] + main[48:96] + rest
            columns = slice((k % 2) * 256, (k % 2) * 256 + 256)
            if first:
                total = total + part[b, half, :, columns]
            part[b, half, :, columns] = total
            if k == 1 and end == TILES:
                core_copies[b].start()

    def stage_two(b):
        core_copies[b].wait_recv()
        for k in range(4):
            value = part[b, core, :, k * 128 : (k + 1) * 128] + crecv[b, :, k * 128 : (k + 1) * 128]
            turned = pltpu.roll(value, 64, 1)
            xs[b, k] = jnp.where(lane < 64, value[0:ROWS], turned[ROWS:])
            xs[b, 4 + k] = jnp.where(lane < 64, turned[0:ROWS], value[ROWS:])
        for copy in x_copies[b]:
            copy.start()

    def stage_three(b):
        value = xs[b, yh * 4 + x]
        for k, copy in enumerate(x_copies[b]):
            copy.wait_recv()
            value = value + xrecv[b, k]
        turned = pltpu.roll(value, 64, 1)
        for i in (0, 1):
            low, high = (value, turned) if i == 0 else (turned, value)
            high = jnp.concatenate([high[16:24], jnp.zeros((8, 128), jnp.float32)], axis=0)
            sums[2 * b + i] = jnp.where(lane[0:16] < 64, low[0:16], high)

    def sum_of(name, inputs):
        b = [name in pair for pair in PAIRS].index(True)
        value = sums[2 * b + PAIRS[b].index(name)]
        for key in inputs:
            owner_copies[key].wait_recv()
            value = value + inbox[INBOX[key]]
        return value

    def send_on(name):
        outbox[INBOX[name]] = sum_of(name, ("B" + name[1:],) if name[0] == "A" else ())
        owner_copies[name].start()
        sent.append(name)

    amp_copy.wait()
    ensure_pack(PLACE["A4"])
    pl.semaphore_wait(barrier, len(greeted))

    for slot in range(LAG):
        ring_start("p", slot)
        ring_start("m", slot)
        y_start()
    for k in range(16):
        ensure_pack(k)

    int_copy.start()
    tables = [
        pltpu.make_async_copy(source, table, table_sem.at[k])
        for k, (source, table) in enumerate(((pair, pair_ref), (occ, occ_ref), (virt, virt_ref)))
    ]
    for copy in tables:
        copy.start()
    for copy in tables:
        copy.wait()

    row24 = lax.broadcasted_iota(jnp.int32, (ROWS, 128), 0)
    occ_pair = jnp.zeros((ROWS, 128), jnp.float32)
    for r in range(ROWS):
        both = pair_ref[r]
        occ_pair = jnp.where(row24 == r, occ_ref[both // NOCC] + occ_ref[both % NOCC], occ_pair)
    virt_pair = jnp.zeros((ROWS, 128), jnp.float32)
    for c in range(MINE):
        row = ab * MINE + c
        virt_pair = jnp.where(lane == c, virt_ref[row // NV] + virt_ref[row % NV], virt_pair)
    den[...] = occ_pair - virt_pair

    int_copy.wait()
    split_columns(FULL * 128, REST)
    splits = {0: (0, 6), 1: (6, 12), 2: (12, 19)}

    waits = {"ring": 0, "batch": 0, "cross": 0}
    sent = []

    def settle(slot, batch):
        while waits["ring"] <= slot:
            for way in ("p", "m"):
                ring[way, waits["ring"]].wait_send()
            waits["ring"] += 1
        while waits["cross"] < state["y_waited"] - 1:
            ycopies[waits["cross"]].wait_send()
            waits["cross"] += 1
        while waits["batch"] <= batch:
            for copy in [core_copies[waits["batch"]]] + x_copies[waits["batch"]]:
                copy.wait_send()
            waits["batch"] += 1

    for slot in range(SLOTS):
        for way in ("p", "m"):
            ring[way, slot].wait_recv()
            ring_start(way, slot + LAG)
        if slot in splits:
            split_range(*splits[slot])
        if slot in BATCHES:
            b = list(BATCHES).index(slot)
            if "B0" in BATCHES[slot]:
                y_wait(7)
            multiply(b, 0, TILES)
            if b == NB - 1:
                stage_two(b)
            if b:
                stage_three(b - 1)
                for name in SEND_ON.get(b - 1, ()):
                    send_on(name)
            if b < NB - 1:
                stage_two(b)
                settle(slot - 3, b - 2)
        else:
            settle(slot - 3, -1)

    for name in sent[:-2]:
        owner_copies[name].wait_send()
    settle(SLOTS - 4, NB - 3)
    total = sum_of("A0", ("B0",) + OWN[:-3])
    stage_three(NB - 1)
    send_on("A1p")
    send_on("A1m")
    settle(SLOTS - 1, NB - 1)
    for copy in ycopies[waits["cross"] :] + [owner_copies[name] for name in sent[-4:]]:
        copy.wait_send()
    for name in ("A1p", "A1m"):
        owner_copies[name].wait_recv()
        total = total + inbox[INBOX[name]]
    turned = pltpu.roll(total, 64, 1)
    ladder = jnp.concatenate([total, turned[0:8]], axis=0)
    out[...] = (ladder / den[...])[:, :MINE]


def per_device(amplitudes, integrals, pair_index, occ_energy, virt_energy):
    dma = pltpu.SemaphoreType.DMA

    def f32(*shape):
        return pltpu.VMEM(shape, jnp.float32)

    def bf16(*shape):
        return pltpu.VMEM(shape, jnp.bfloat16)

    return pl.pallas_call(
        kernel,
        out_shape=jax.ShapeDtypeStruct((ROWS, MINE), jnp.float32),
        in_specs=[pl.BlockSpec(memory_space=pl.ANY)] * 5,
        out_specs=pl.BlockSpec(memory_space=pltpu.VMEM),
        scratch_shapes=[
            f32(ROWS, COLS), f32(WINDOW, EACH), bf16(4, WIDE, 256), bf16(4, WIDE, 256),
            f32(16, 8, SENT), f32(8, 8, SENT), f32(SLOTS, 8, SENT), f32(SLOTS, 8, SENT),
            bf16(96, WIDE), f32(NB, 2, 48, 512), f32(NB, 48, 512), f32(NB, 8, ROWS, 128), f32(NB, 7, ROWS, 128),
            f32(2 * NB, 16, 128), f32(len(INBOX), 16, 128), f32(len(INBOX), 16, 128), f32(ROWS, 128),
            pltpu.SMEM((ROWS,), jnp.int32), pltpu.SMEM((NOCC,), jnp.float32), pltpu.SMEM((NV,), jnp.float32),
            dma, dma, dma((3,)), dma((8,)), dma((8,)), dma((SLOTS,)), dma((SLOTS,)), dma((SLOTS,)), dma((SLOTS,)),
            dma((NB,)), dma((NB,)), dma((NB, 7)), dma((NB, 7)), dma((len(INBOX),)), dma((len(INBOX),)),
        ],
        compiler_params=pltpu.CompilerParams(
            collective_id=0, has_side_effects=True, vmem_limit_bytes=60 * 2**20
        ),
        cost_estimate=pl.CostEstimate(flops=4_700_000_000, bytes_accessed=12_000_000, transcendentals=0),
        name="ladder",
    )(amplitudes, integrals, pair_index, occ_energy, virt_energy)


def solution(mesh):
    return jax.shard_map(
        per_device,
        mesh=mesh,
        in_specs=(P("cd", "ab"), P(None, ("ab", "cd")), P("cd"), P(), P()),
        out_specs=P("cd", "ab"),
        check_vma=False,
    )
```
